256 devices in a mesh: attn: 64 (over x, z_hi, y, core), ffn: 4 (over z_lo).
Axes of the slice: x: 4, y: 4, z: 8 (z_hi: 2, z_lo: 4; z = z_hi * 4 + z_lo), core: 2. Of those that a mesh axis runs over, the one named last changes fastest.
Arguments:
- queries: bfloat16 [512, 8192], P('attn', 'ffn'), may hold values from -132 to 132
- cache_keys: bfloat16 [512, 512, 512], P('attn', None, 'ffn'), may hold values from -6 to 6
- value_cache: bfloat16 [512, 512, 512], P('attn', None, 'ffn'), may hold values from -6 to 6
- new_keys: bfloat16 [512, 512], P('attn', 'ffn'), may hold values from -6 to 6
- token_values: bfloat16 [512, 512], P('attn', 'ffn'), may hold values from -6 to 6
- lengths: int32 [512], P('attn'), may hold values from 1 to 512, 87381 in all
- norm_gain: float32 [8192], P('ffn'), may hold values from 0.1 to 1.9
- w_gate: bfloat16 [8192, 40960], P('ffn', 'attn'), may hold values from -0.0625 to 0.0625
- w_up: bfloat16 [8192, 40960], P('ffn', 'attn'), may hold values from -0.0625 to 0.0625
- w_down: bfloat16 [40960, 8192], P('attn', 'ffn'), may hold values from -0.03125 to 0.03125
Outputs:
- attn_out: bfloat16 [512, 8192], P('attn', 'ffn')
- ffn_out: bfloat16 [512, 8192], P('attn', 'ffn')
The draws below stay inside these ranges and needn't reach their ends.
All inputs are finite; a program needn't handle non-finite values. No bound on the sum of `lengths` on one device may be relied on, other than what follows from the above.
Results may differ from the reference program's by a relative error of at most 0.013.
Values may be sent and summed in bfloat16 or wider, within the bound.
A program may use at most 128 MiB of HBM per device.

```python
import math
import jax
import jax.numpy as jnp
import numpy as np
from jax import lax

HEAD_DIM = 128
QUERY_HEADS = 64
KEY_VALUE_HEADS = 4
D = 8192
FF = 40960
MAX_LENGTH = 512
REQUEST_COUNT = 512
TOTAL_LEN = 87381


def shared_new_keys(key):
    return jnp.clip(jax.random.normal(key, (REQUEST_COUNT, KEY_VALUE_HEADS * HEAD_DIM), jnp.float32), -6.0, 6.0)


def draw_new_keys(key, part):
    return shared_new_keys(key).astype(jnp.bfloat16)


def draw_queries(key, part):
    key = jax.random.fold_in(key, 11)
    drawn_sample = jnp.clip(jax.random.normal(key, (REQUEST_COUNT, QUERY_HEADS * HEAD_DIM), jnp.float32), -6.0, 6.0)
    return drawn_sample.astype(jnp.bfloat16)


def draw_cache_keys(key, part):
    key = jax.random.fold_in(key, 12)
    drawn_sample = jnp.clip(jax.random.normal(key, (REQUEST_COUNT, MAX_LENGTH, KEY_VALUE_HEADS * HEAD_DIM), jnp.float32), -6.0, 6.0)
    return drawn_sample.astype(jnp.bfloat16)


def block_scale(stream_key, extent, split, least, high):
    loudness, own = 1.0, jax.random.fold_in(stream_key, 6)
    for dim, parts in split:
        steps = jnp.exp(jax.random.uniform(jax.random.fold_in(own, dim), (parts,), jnp.float32, least / len(split), high / len(split)))
        loudness = loudness * jnp.repeat(steps, extent[dim] // parts).reshape([-1 if axis == dim else 1 for axis in range(len(extent))])
    return loudness


def profile(count, total, most, skew):
    portions = [(1 << 20) // math.isqrt(rank ** skew) + 1 for rank in range(2, count + 1)]
    spare, given = total - most - (count - 1), [1] * (count - 1)
    while spare > 0:
        movable = [i for i in range(count - 1) if given[i] < most]
        mass, budget = sum([portions[i] for i in movable]), spare
        for i in movable:
            addition = min(most - given[i], max(1, budget * portions[i] // mass), spare)
            given[i] = given[i] + addition
            spare = spare - addition
    return np.array([most] + given)


def uneven(rng, amount, total, bound, slope):
    if amount == 2:
        one = jax.random.randint(rng, (), max(1, total - bound), min(bound, total - 1) + 1)
        return jnp.stack([one, total - one])
    tallies = jnp.asarray(profile(amount, total, bound, slope), jnp.int32)
    twos = (amount - 1) // 2
    giver, taker = tallies[1:1 + 2 * twos:2], tallies[2:2 + 2 * twos:2]
    margin = jnp.minimum(giver - 1, bound - taker)
    shifted = jax.random.randint(jax.random.fold_in(rng, 1), (twos,), 0, 1 << 20) % (margin + 1)
    tallies = tallies.at[1:1 + 2 * twos:2].set(giver - shifted).at[2:2 + 2 * twos:2].set(taker + shifted)
    return tallies[jax.random.permutation(jax.random.fold_in(rng, 2), amount)]


def bell_draw(stream_key, shape, width, reach, cuts=(), held_as=jnp.bfloat16):
    gain = block_scale(stream_key, shape, cuts, -0.22, 0.18) if cuts else 1.0
    result = jax.random.normal(stream_key, shape, jnp.float32) * width * gain
    return jnp.minimum(jnp.maximum(result, -reach), reach).astype(held_as)


def setup_inputs(seed: int = 0) -> dict:
    splits = jax.random.split(jax.random.key(seed), 11)
    return {
        "queries": draw_queries(jax.random.fold_in(splits[10], 71), 0),
        "cache_keys": draw_cache_keys(jax.random.fold_in(splits[10], 71), 0),
        "value_cache": bell_draw(splits[2], (REQUEST_COUNT, MAX_LENGTH, KEY_VALUE_HEADS * HEAD_DIM), 1.0, 6.0, ((0, 64), (2, 4))),
        "new_keys": draw_new_keys(jax.random.fold_in(splits[10], 71), 0),
        "token_values": bell_draw(splits[4], (REQUEST_COUNT, KEY_VALUE_HEADS * HEAD_DIM), 1.0, 6.0, ((0, 64), (1, 4))),
        "lengths": uneven(splits[5], REQUEST_COUNT, TOTAL_LEN, MAX_LENGTH, 2).astype(jnp.int32),
        "norm_gain": jnp.clip(1.0 + 0.18 * jax.random.normal(splits[6], (D,), jnp.float32), 0.1, 1.9),
        "w_gate": bell_draw(splits[7], (D, FF), D ** -0.5, 0.0625, ((0, 4), (1, 64))),
        "w_up": bell_draw(splits[8], (D, FF), D ** -0.5, 0.0625, ((0, 4), (1, 64))),
        "w_down": bell_draw(splits[9], (FF, D), FF ** -0.5, 0.03125, ((0, 64), (1, 4))),
    }


def attend_request(inputs):
    row_query, row_keys, row_values, fresh_key, fresh_value, length = inputs
    group_width = QUERY_HEADS // KEY_VALUE_HEADS
    scaling = 1.0 / HEAD_DIM ** 0.5
    heads_query = row_query.astype(jnp.float32).reshape(KEY_VALUE_HEADS, group_width, HEAD_DIM)
    block_keys = row_keys.astype(jnp.float32).reshape(MAX_LENGTH, KEY_VALUE_HEADS, HEAD_DIM)
    block_values = row_values.astype(jnp.float32).reshape(MAX_LENGTH, KEY_VALUE_HEADS, HEAD_DIM)
    self_key = fresh_key.astype(jnp.float32).reshape(KEY_VALUE_HEADS, HEAD_DIM)
    self_value = fresh_value.astype(jnp.float32).reshape(KEY_VALUE_HEADS, HEAD_DIM)
    scores = jnp.einsum('kgd,jkd->kgj', heads_query, block_keys) * scaling
    own_score = jnp.einsum('kgd,kd->kg', heads_query, self_key) * scaling
    live_mask = jnp.arange(MAX_LENGTH, dtype=jnp.int32) < length
    scores = jnp.where(live_mask[None, None, :], scores, -1e+30)
    largest = jnp.maximum(lax.optimization_barrier(jnp.max(scores, axis=-1)), own_score)
    weights = jnp.where(live_mask[None, None, :], jnp.exp(scores - largest[..., None]), 0.0)
    own_weight = jnp.exp(own_score - largest)
    denominator = lax.optimization_barrier(jnp.sum(weights, axis=-1)) + own_weight
    probs = (weights / denominator[..., None]).astype(jnp.bfloat16)
    own_prob = (own_weight / denominator).astype(jnp.bfloat16)
    attended = jnp.einsum('kgj,jkd->kgd', probs.astype(jnp.float32), block_values)
    attended = attended + own_prob.astype(jnp.float32)[..., None] * self_value[:, None, :]
    return attended.reshape(QUERY_HEADS * HEAD_DIM).astype(jnp.bfloat16)

def reference(queries, cache_keys, value_cache, new_keys, token_values, lengths, norm_gain, w_gate, w_up, w_down):
    attn_out = lax.map(attend_request, (queries, cache_keys, value_cache, new_keys, token_values, lengths))
    features = attn_out.astype(jnp.float32)
    mean_square = lax.optimization_barrier(jnp.mean(features * features, axis=-1, keepdims=True))
    normed = (features * lax.rsqrt(mean_square + 1e-05) * norm_gain[None, :]).astype(jnp.bfloat16)
    gate = jnp.dot(normed, w_gate, preferred_element_type=jnp.float32)
    up_sum = jnp.dot(normed, w_up, preferred_element_type=jnp.float32)
    hidden = (jax.nn.silu(gate) * up_sum).astype(jnp.bfloat16)
    ffn_out = jnp.dot(hidden, w_down, preferred_element_type=jnp.float32).astype(jnp.bfloat16)
    return (attn_out, ffn_out)
```

```python
import functools

import jax
import jax.numpy as jnp
from jax import lax
from jax.experimental import pallas as pl
from jax.experimental.pallas import tpu as pltpu
from jax.sharding import PartitionSpec as P

MESH = pl.DeviceIdType.MESH
F32, BF16 = jnp.float32, jnp.bfloat16
D = 8192
CHUNKS = 8
ROWS = 64
PART = 32
UNITS = 640
LAST = 3


def chunk_of(j, x, zh):
    i = j // 2
    dx = i + (i // 2) * (5 - 2 * i)
    flip = (j + (j + 6) // 8) % 2
    return dx, flip, ((x + dx) % 4) * 2 + (zh + flip) % 2


def kernel(
    q_ref, nk_ref, tv_ref, len_ref, gain_ref, k_hbm, v_hbm, wg_hbm, wu_hbm, wd_hbm,
    attn_ref, out_ref,
    kbuf, vbuf, wgu, wd, qs, os, ssr, xblk, xall, part, sbuf, rbuf, hbuf, cs, cr, acc, xcs, xcr, zcs, zcr,
    load_sem, ss_send, ss_recv, z_send, z_recv, y_send, y_recv, x_send, x_recv, f_send, f_recv,
    r_send, r_recv, h_send, h_recv, c_send, c_recv, xc_send, xc_recv, zc_send, zc_recv,
):
    a = lax.axis_index("attn")
    zl = lax.axis_index("ffn")
    c = a % 2
    y = (a // 2) % 4
    zh = (a // 8) % 2
    x = a // 16
    slot = y * 2 + c

    def at(x_, zh_, slot_, zl_=None):
        return {"attn": (x_ * 2 + zh_) * 8 + slot_, "ffn": zl if zl_ is None else zl_}

    sibling = at(x, zh, y * 2 + (1 - c))
    partner = at(x, 1 - zh, slot)

    def remote(src, dst, send, recv, device):
        return pltpu.make_async_remote_copy(
            src_ref=src, dst_ref=dst, send_sem=send, recv_sem=recv, device_id=device, device_id_type=MESH
        )

    loads = [
        pltpu.make_async_copy(k_hbm, kbuf, load_sem.at[0]),
        pltpu.make_async_copy(v_hbm, vbuf, load_sem.at[1]),
        pltpu.make_async_copy(wg_hbm, wgu.at[:, pl.ds(0, UNITS)], load_sem.at[2]),
        pltpu.make_async_copy(wu_hbm, wgu.at[:, pl.ds(UNITS, UNITS)], load_sem.at[3]),
        pltpu.make_async_copy(wd_hbm, wd, load_sem.at[4]),
    ]
    for load in loads:
        load.start()

    barrier = pltpu.get_barrier_semaphore()
    peers = [at(x, zh, (slot + d) % 8) for d in range(1, 8)]
    peers += [at((x + d) % 4, zh, slot) for d in range(1, 4)]
    peers += [at(x, zh, slot, (zl + d) % 4) for d in range(1, 4)]
    peers += [partner]
    for peer in peers:
        pl.semaphore_signal(barrier, inc=1, device_id=peer, device_id_type=MESH)

    qf = q_ref[...].astype(F32)
    for g in range(16):
        qs[pl.ds(g * 8, 8), :] = qf[:, g * 128 : (g + 1) * 128]
    nk = nk_ref[...].astype(F32)
    tv = tv_ref[...].astype(F32)
    loads[0].wait()
    loads[1].wait()
    scaling = 1.0 / 128**0.5
    position = lax.broadcasted_iota(jnp.int32, (16, 512), 1)
    for r in range(8):
        q = qs[pl.ds(r, 16, stride=8), :]
        scores = lax.dot_general(
            q.astype(BF16), kbuf[r], (((1,), (1,)), ((), ())), preferred_element_type=F32
        ) * scaling
        own = jnp.sum(q * nk[r : r + 1, :], axis=1, keepdims=True) * scaling
        live = position < len_ref[r]
        scores = jnp.where(live, scores, -1e30)
        largest = jnp.maximum(jnp.max(scores, axis=1, keepdims=True), own)
        weights = jnp.where(live, jnp.exp(scores - largest), 0.0)
        own_weight = jnp.exp(own - largest)
        total = jnp.sum(weights, axis=1, keepdims=True) + own_weight
        probs = (weights / total).astype(BF16)
        own_prob = (own_weight / total).astype(BF16).astype(F32)
        out = jnp.dot(probs, vbuf[r], preferred_element_type=F32)
        os[pl.ds(r, 16, stride=8), :] = out + own_prob * tv[r : r + 1, :]
    attn = jnp.concatenate([os[pl.ds(g * 8, 8), :] for g in range(16)], axis=1).astype(BF16)
    attn_ref[...] = attn
    feats = attn.astype(F32)
    ssr[zl] = jnp.broadcast_to(jnp.sum(feats * feats, axis=1, keepdims=True), (8, 128))

    pl.semaphore_wait(barrier, len(peers))

    def ss_copy(d):
        return remote(ssr.at[zl], ssr.at[zl], ss_send.at[d], ss_recv.at[zl], at(x, zh, slot, (zl + d) % 4))

    def ss_from(d):
        s = (zl + d) % 4
        return remote(ssr.at[s], ssr.at[s], ss_send.at[d], ss_recv.at[s], at(x, zh, slot, s))

    for d in range(1, 4):
        ss_copy(d).start()
    for d in range(1, 4):
        ss_from(d).wait_recv()
    squares = ssr[0] + ssr[1] + ssr[2] + ssr[3]
    scale = lax.rsqrt(squares[:, :1] / D + 1e-05)
    normed = feats * scale * gain_ref[...]
    xblk[0, slot] = jnp.concatenate([normed[:, :1024], normed[:, 1024:]], axis=0).astype(BF16)

    z_copy = remote(xblk.at[0, slot], xblk.at[1, slot], z_send, z_recv, partner)
    z_copy.start()

    def y_copy(w, d):
        return remote(
            xblk.at[w, slot], xblk.at[w, slot], y_send.at[w, d], y_recv.at[w, slot], at(x, zh, (slot + d) % 8)
        )

    def y_from(w, d):
        s = (slot + d) % 8
        return remote(xblk.at[w, s], xblk.at[w, s], y_send.at[w, d], y_recv.at[w, s], at(x, zh, s))

    def own_chunk(w):
        return x * 2 + (zh + w) % 2

    def x_copy(w, d):
        n = own_chunk(w)
        return remote(
            xall.at[n, c], xall.at[n, c], x_send.at[w, d], x_recv.at[n], at((x + d) % 4, zh, slot)
        )

    def assemble(w):
        n = own_chunk(w)
        for d in range(1, 8):
            y_from(w, d).wait_recv()
        for b in range(4):
            first = xblk[w, 2 * b].astype(F32)
            second = xblk[w, 2 * b + 1].astype(F32)
            for h in range(2):
                pair = [first[8 * h : 8 * h + 8], second[8 * h : 8 * h + 8]]
                xall[n, h, pl.ds(16 * b, 16), :] = jnp.concatenate(pair, axis=0).astype(BF16)
        for d in (1, 3, 2):
            x_copy(w, d).start()

    for d in range(1, 8):
        y_copy(0, d).start()
    z_copy.wait_recv()
    for d in range(1, 8):
        y_copy(1, d).start()
    assemble(0)
    for load in loads[2:]:
        load.wait()

    positions = [zl, LAST - zl]
    nexts = [at(x, zh, slot, (zl + 1) % 4), at(x, zh, slot, (zl + 3) % 4)]
    backs = [nexts[1], nexts[0]]

    def r_copy(dr, j):
        return remote(sbuf.at[dr, j], rbuf.at[dr, j], r_send.at[dr, j], r_recv.at[dr, j], nexts[dr])

    def h_copy(dr, j):
        piece = hbuf.at[j, pl.ds(dr * PART, PART)]
        return remote(piece, piece, h_send.at[dr, j], h_recv.at[dr, j], backs[dr])

    def forward(j):
        n = chunk_of(j, x, zh)[2]
        return remote(xall.at[n, c], xall.at[n, c], f_send.at[j], f_recv.at[j], sibling)

    def forwarded(j):
        n = chunk_of(j, x, zh)[2]
        return remote(xall.at[n, 1 - c], xall.at[n, 1 - c], f_send.at[j], f_recv.at[j], sibling)

    def x_from(j):
        dx, _, n = chunk_of(j, x, zh)
        return remote(xall.at[n, c], xall.at[n, c], f_send.at[j], x_recv.at[n], at((x + dx) % 4, zh, slot))

    def c_copy(j, d):
        s = (slot + d) % 8
        return remote(cs.at[j, s], cr.at[j, slot], c_send.at[j, d], c_recv.at[j, slot], at(x, zh, s))

    def c_from(j, d):
        s = (slot + d) % 8
        return remote(cs.at[j, s], cr.at[j, s], c_send.at[j, d], c_recv.at[j, s], at(x, zh, s))

    def xc_copy(flip, dx):
        k = dx - 1
        return remote(
            xcs.at[flip, k], xcr.at[flip, k], xc_send.at[flip, k], xc_recv.at[flip, k], at((x + dx) % 4, zh, slot)
        )

    def body(i, carry):
        for dr in range(2):
            p = positions[dr]
            j = i - p

            @pl.when((p > 0) & (j >= 0) & (j < CHUNKS))
            def _():
                r_copy(dr, j).wait_recv()
                sums = part[j, pl.ds(dr * PART, PART), :] + rbuf[dr, j].astype(F32)

                @pl.when(p < LAST)
                def _():
                    sbuf[dr, j] = sums.astype(BF16)
                    r_copy(dr, j).start()

                @pl.when(p == LAST)
                def _():
                    gate, up = sums[:, :UNITS], sums[:, UNITS:]
                    hidden = gate / (1.0 + jnp.exp(-gate)) * up
                    hbuf[j, pl.ds(dr * PART, PART), :] = hidden.astype(BF16)
                    h_copy(dr, j).start()

        for dr in range(2):
            p = positions[dr]
            j = i - (2 * LAST - p)

            @pl.when((p < LAST) & (j >= 0) & (j < CHUNKS))
            def _():
                h_copy(dr, j).wait_recv()

                @pl.when(p > 0)
                def _():
                    h_copy(dr, j).start()

        @pl.when(i < CHUNKS)
        def _():
            @pl.when(i >= 2)
            def _():
                forwarded(i).wait_recv()

            n = chunk_of(i, x, zh)[2]
            for t in range(5):
                cols = pl.ds(t * 256, 256)
                part[i, :, cols] = jnp.dot(
                    xall[n, 0], wgu[pl.ds(0, 1024), cols], preferred_element_type=F32
                ) + jnp.dot(xall[n, 1], wgu[pl.ds(1024, 1024), cols], preferred_element_type=F32)
            for dr in range(2):

                @pl.when(positions[dr] == 0)
                def _():
                    sbuf[dr, i] = part[i, pl.ds(dr * PART, PART), :].astype(BF16)
                    r_copy(dr, i).start()

        @pl.when(i == 0)
        def _():
            assemble(1)

        @pl.when((i >= 1) & (i < CHUNKS - 1))
        def _():
            x_from(i + 1).wait_recv()
            forward(i + 1).start()

        j = i - 2 * LAST

        @pl.when((j >= 0) & (j < CHUNKS))
        def _():
            hidden = hbuf[j]
            for t in range(4):
                left = jnp.dot(hidden, wd[:, pl.ds(t * 256, 256)], preferred_element_type=F32)
                right = jnp.dot(hidden, wd[:, pl.ds(1024 + t * 256, 256)], preferred_element_type=F32)
                for b in range(8):
                    block = jnp.concatenate([left[b * 8 : b * 8 + 8], right[b * 8 : b * 8 + 8]], axis=0)
                    cs[j, b, :, pl.ds(t * 256, 256)] = block.astype(BF16)
            for d in range(1, 8):
                c_copy(j, d).start()
            cr[j, slot] = cs[j, slot]

        m = i - 2 * LAST - 1

        @pl.when(m >= 0)
        def _():
            for d in range(1, 8):
                c_from(m, d).wait_recv()
            total = cr[m, 0].astype(F32)
            for b in range(1, 8):
                total = total + cr[m, b].astype(F32)
            dx, flip, _ = chunk_of(m, x, zh)

            @pl.when(m < 2)
            def _():
                acc[flip] = total

            @pl.when(m >= 2)
            def _():
                xcs[flip, dx - 1] = total.astype(BF16)
                xc_copy(flip, dx).start()

        return carry

    lax.fori_loop(0, CHUNKS + 2 * LAST + 1, body, 0)

    sums = []
    zc_copy = remote(zcs, zcr, zc_send, zc_recv, partner)
    for flip in (1, 0):
        for dx in range(1, 4):
            xc_copy(flip, dx).wait_recv()
        total = acc[flip]
        for dx in range(1, 4):
            total = total + xcr[flip, dx - 1].astype(F32)
        if flip == 1:
            zcs[...] = total.astype(BF16)
            zc_copy.start()
    zc_copy.wait_recv()
    total = total + zcr[...].astype(F32)
    out_ref[...] = jnp.concatenate([total[:8], total[8:]], axis=1).astype(BF16)

    zc_copy.wait_send()
    z_copy.wait_send()
    for d in range(1, 4):
        ss_copy(d).wait_send()
        for w in range(2):
            x_copy(w, d).wait_send()
            xc_copy(w, d).wait_send()
    for d in range(1, 8):
        for w in range(2):
            y_copy(w, d).wait_send()

    def drain(j, carry):
        @pl.when(j >= 2)
        def _():
            forward(j).wait_send()

        for d in range(1, 8):
            c_copy(j, d).wait_send()
        for dr in range(2):

            @pl.when(positions[dr] < LAST)
            def _():
                r_copy(dr, j).wait_send()

            @pl.when(positions[dr] > 0)
            def _():
                h_copy(dr, j).wait_send()

        return carry

    lax.fori_loop(0, CHUNKS, drain, 0)


def local(queries, cache_keys, value_cache, new_keys, token_values, lengths, norm_gain, w_gate, w_up, w_down):
    vmem = pl.BlockSpec(memory_space=pltpu.VMEM)
    hbm = pl.BlockSpec(memory_space=pl.ANY)
    dma = pltpu.SemaphoreType.DMA
    return pl.pallas_call(
        kernel,
        out_shape=(jax.ShapeDtypeStruct((8, 2048), BF16), jax.ShapeDtypeStruct((8, 2048), BF16)),
        in_specs=[vmem, vmem, vmem, pl.BlockSpec(memory_space=pltpu.SMEM), vmem] + [hbm] * 5,
        out_specs=(vmem, vmem),
        scratch_shapes=[
            pltpu.VMEM((8, 512, 128), BF16),
            pltpu.VMEM((8, 512, 128), BF16),
            pltpu.VMEM((2048, 2 * UNITS), BF16),
            pltpu.VMEM((UNITS, 2048), BF16),
            pltpu.VMEM((128, 128), F32),
            pltpu.VMEM((128, 128), F32),
            pltpu.VMEM((4, 8, 128), F32),
            pltpu.VMEM((2, 8, 16, 1024), BF16),
            pltpu.VMEM((CHUNKS, 2, ROWS, 1024), BF16),
            pltpu.VMEM((CHUNKS, ROWS, 2 * UNITS), F32),
            pltpu.VMEM((2, CHUNKS, PART, 2 * UNITS), BF16),
            pltpu.VMEM((2, CHUNKS, PART, 2 * UNITS), BF16),
            pltpu.VMEM((CHUNKS, ROWS, UNITS), BF16),
            pltpu.VMEM((CHUNKS, 8, 16, 1024), BF16),
            pltpu.VMEM((CHUNKS, 8, 16, 1024), BF16),
            pltpu.VMEM((2, 16, 1024), F32),
            pltpu.VMEM((2, 3, 16, 1024), BF16),
            pltpu.VMEM((2, 3, 16, 1024), BF16),
            pltpu.VMEM((16, 1024), BF16),
            pltpu.VMEM((16, 1024), BF16),
            dma((5,)),
            dma((4,)), dma((4,)),
            dma, dma,
            dma((2, 8)), dma((2, 8)),
            dma((2, 4)), dma((CHUNKS,)),
            dma((CHUNKS,)), dma((CHUNKS,)),
            dma((2, CHUNKS)), dma((2, CHUNKS)),
            dma((2, CHUNKS)), dma((2, CHUNKS)),
            dma((CHUNKS, 8)), dma((CHUNKS, 8)),
            dma((2, 3)), dma((2, 3)),
            dma, dma,
        ],
        compiler_params=pltpu.CompilerParams(
            collective_id=0, has_side_effects=True, vmem_limit_bytes=50 * 1024 * 1024
        ),
    )(queries, new_keys, token_values, lengths, norm_gain.reshape(1, 2048), cache_keys, value_cache, w_gate, w_up, w_down)


def solution(mesh):
    in_specs = (
        P("attn", "ffn"),
        P("attn", None, "ffn"),
        P("attn", None, "ffn"),
        P("attn", "ffn"),
        P("attn", "ffn"),
        P("attn"),
        P("ffn"),
        P("ffn", "attn"),
        P("ffn", "attn"),
        P("attn", "ffn"),
    )
    out_specs = (P("attn", "ffn"), P("attn", "ffn"))
    return jax.shard_map(local, mesh=mesh, in_specs=in_specs, out_specs=out_specs, check_vma=False)
```

```python
import functools

import jax
import jax.numpy as jnp
from jax import lax
from jax.experimental import pallas as pl
from jax.experimental.pallas import tpu as pltpu
from jax.sharding import PartitionSpec as P

MESH = pl.DeviceIdType.MESH
F32, BF16 = jnp.float32, jnp.bfloat16
D = 8192
CHUNKS = 8
ROWS = 64
PART = 32
UNITS = 640
AT_ENDS = 1


def from_on(j, k):
    return (j + 8 - k) // 8


def chunk_of(j, x, zh):
    dx = from_on(j, 2) + from_on(j, 3) - from_on(j, 4) + from_on(j, 5) + from_on(j, 6)
    flip = from_on(j, 1) - from_on(j, 2) + from_on(j, 4) - from_on(j, 7)
    return dx, flip, ((x + dx) % 4) * 2 + (zh + flip) % 2


def kernel(
    q_hbm, nk_hbm, tv_hbm, len_hbm, gain_hbm, k_hbm, v_hbm, wg_hbm, wu_hbm, wd_hbm,
    attn_ref, out_ref,
    q_ref, nk_ref, tv_ref, len_ref, gain_ref, kbuf, vbuf, wgu, wd,
    qs, os, col, scales, sums, ssr, xblk, xall, xg, part, pout, pin, mout, min_, hbuf, cs, sr, cy, cr, acc, xcs, xcr, zcs, zcr,
    load_sem, ss_send, ss_recv, z_send, z_recv, y_send, y_recv, x_send, x_recv, f_send, f_recv,
    p_send, p_recv, m_send, m_recv, e_recv, h_send, h_recv, s_send, s_recv, c_send, c_recv, xc_send, xc_recv, zc_send, zc_recv,
):
    a = lax.axis_index("attn")
    zl = lax.axis_index("ffn")
    c = a % 2
    y = (a // 2) % 4
    zh = (a // 8) % 2
    x = a // 16
    slot = y * 2 + c

    def at(x_, zh_, slot_, zl_=None):
        return {"attn": (x_ * 2 + zh_) * 8 + slot_, "ffn": zl if zl_ is None else zl_}

    sibling = at(x, zh, y * 2 + (1 - c))
    partner = at(x, 1 - zh, slot)

    def remote(src, dst, send, recv, device):
        return pltpu.make_async_remote_copy(
            src_ref=src, dst_ref=dst, send_sem=send, recv_sem=recv, device_id=device, device_id_type=MESH
        )

    pairs = [
        (q_hbm, q_ref), (nk_hbm, nk_ref), (len_hbm, len_ref), (k_hbm, kbuf), (tv_hbm, tv_ref), (v_hbm, vbuf), (gain_hbm, gain_ref),
        (wg_hbm, wgu.at[:, pl.ds(0, UNITS)]), (wu_hbm, wgu.at[:, pl.ds(UNITS, UNITS)]), (wd_hbm, wd),
    ]
    loads = [pltpu.make_async_copy(src, dst, load_sem.at[n]) for n, (src, dst) in enumerate(pairs)]
    for load in loads[:7]:
        load.start()

    barrier = pltpu.get_barrier_semaphore()
    peers = [at(x, zh, (slot + d) % 8) for d in range(1, 8)]
    peers += [at((x + d) % 4, zh, slot) for d in range(1, 4)]
    peers += [at(x, zh, slot, (zl + d) % 4) for d in range(1, 4)]
    peers += [at((x + d) % 4, 1 - zh, slot) for d in range(4)]
    for peer in peers:
        pl.semaphore_signal(barrier, inc=1, device_id=peer, device_id_type=MESH)

    for load in loads[:7]:
        load.wait()
    for load in loads[7:]:
        load.start()
    qf = q_ref[...].astype(F32)
    for g in range(16):
        qs[pl.ds(g * 8, 8), :] = qf[:, g * 128 : (g + 1) * 128]
    nk = nk_ref[...].astype(F32)
    tv = tv_ref[...].astype(F32)
    scaling = 1.0 / 128**0.5
    position = lax.broadcasted_iota(jnp.int32, (16, 512), 1)
    for r in range(8):
        q = qs[pl.ds(r, 16, stride=8), :]
        scores = lax.dot_general(
            q.astype(BF16), kbuf[r], (((1,), (1,)), ((), ())), preferred_element_type=F32
        ) * scaling
        own = jnp.sum(q * nk[r : r + 1, :], axis=1, keepdims=True) * scaling
        live = position < len_ref[r]
        scores = jnp.where(live, scores, -1e30)
        largest = jnp.maximum(jnp.max(scores, axis=1, keepdims=True), own)
        weights = jnp.where(live, jnp.exp(scores - largest), 0.0)
        own_weight = jnp.exp(own - largest)
        total = jnp.sum(weights, axis=1, keepdims=True) + own_weight
        probs = (weights / total).astype(BF16)
        own_prob = (own_weight / total).astype(BF16).astype(F32)
        out = jnp.dot(probs, vbuf[r], preferred_element_type=F32)
        os[pl.ds(r, 16, stride=8), :] = out + own_prob * tv[r : r + 1, :]
    attn = jnp.concatenate([os[pl.ds(g * 8, 8), :] for g in range(16)], axis=1).astype(BF16)
    attn_ref[...] = attn
    feats = attn.astype(F32)
    xblk[0, slot] = jnp.concatenate([feats[:, :1024], feats[:, 1024:]], axis=0).astype(BF16)
    col[...] = jnp.zeros_like(col)

    pl.semaphore_wait(barrier, len(peers))

    z_copy = remote(xblk.at[0, slot], xblk.at[1, slot], z_send, z_recv, partner)
    z_copy.start()

    def y_copy(w, d):
        return remote(
            xblk.at[w, slot], xblk.at[w, slot], y_send, y_recv.at[w], at(x, zh, (slot + d) % 8)
        )

    def wait_send(ref, sem):
        remote(ref, ref, sem, sem, sibling).wait_send()

    def wait_recv(ref, sem):
        remote(ref, ref, sem, sem, sibling).wait_recv()

    def own_chunk(w):
        return x * 2 + (zh + w) % 2

    def x_copy(w, d):
        n = own_chunk(w)
        return remote(
            xall.at[n, c], xall.at[n, c], x_send, x_recv.at[n], at((x + d) % 4, zh, slot)
        )

    def assemble(w):
        n = own_chunk(w)
        wait_recv(xblk.at[w, pl.ds(0, 7)], y_recv.at[w])
        for b in range(4):
            first = xblk[w, 2 * b].astype(F32)
            second = xblk[w, 2 * b + 1].astype(F32)
            for h in range(2):
                pair = [first[8 * h : 8 * h + 8], second[8 * h : 8 * h + 8]]
                xall[n, h, pl.ds(16 * b, 16), :] = jnp.concatenate(pair, axis=0).astype(BF16)
        for d in range(1, 4):
            x_copy(w, d).start()

    for d in range(1, 8):
        y_copy(0, d).start()
    assemble(0)
    z_copy.wait_recv()
    for d in range(1, 8):
        y_copy(1, d).start()
    for load in loads[7:]:
        load.wait()

    side = zl // 2
    middle = zl * (3 - zl) // 2
    here = at(x, zh, slot, 1 + side)
    across = at(x, zh, slot, 2 - side)
    near_end = at(x, zh, slot, 3 * side)
    far_end = at(x, zh, slot, 3 - 3 * side)

    def p_copy(j, half, to):
        return remote(pout.at[2 * j + half], pin.at[2 * j + half], p_send, p_recv.at[j, half], to)

    def m_copy(j):
        return remote(mout.at[j], min_.at[j], m_send, m_recv.at[j], across)

    def ss_copy(j, to):
        return remote(ssr.at[4 * j + zl], ssr.at[4 * j + zl], ss_send, ss_recv.at[j], to)

    def h_copy(j, half, n, to):
        piece = hbuf.at[j, half]
        return remote(piece, piece, h_send.at[n], h_recv.at[j], to)

    def end_h_copy(j):
        piece = hbuf.at[j, 1 - side]
        return remote(piece, piece, h_send.at[0], e_recv.at[j], here)

    def activate(j):
        wait_recv(ssr.at[pl.ds(0, 3)], ss_recv.at[j])
        squares = ssr[4 * j] + ssr[4 * j + 1] + ssr[4 * j + 2] + ssr[4 * j + 3]
        scale = lax.rsqrt(squares[:1] / D + 1e-05)
        scales[...] = jnp.broadcast_to(scale, (128, 128)).T
        scale = scales[pl.ds(pl.multiple_of((1 - side) * PART, PART), PART), :][:, :1]
        wait_recv(pin.at[0], p_recv.at[j, 1 - side])
        sums[...] = part[j, 1 - side] + pin[2 * j + 1 - side].astype(F32)

        @pl.when(middle == 1)
        def _():
            wait_recv(min_.at[j], m_recv.at[j])
            sums[...] += min_[j].astype(F32)

        gate, up = sums[:, pl.ds(0, UNITS)] * scale, sums[:, pl.ds(UNITS, UNITS)] * scale
        hidden = gate / (1.0 + jnp.exp(-gate)) * up
        hbuf[j, 1 - side] = hidden.astype(BF16)

    def forward(j):
        n = chunk_of(j, x, zh)[2]
        return remote(xall.at[n, c], xall.at[n, c], f_send, f_recv.at[j], sibling)

    def s_copy(j):
        return remote(cs.at[j, 1 - c], sr.at[j], s_send, s_recv.at[j], sibling)

    def c_copy(j, d):
        to = (y + d) % 4
        return remote(cy.at[j, to], cr.at[j, y], c_send, c_recv.at[j], at(x, zh, to * 2 + c))

    def xc_copy(dx):
        return remote(xcs.at[dx - 1], xcr.at[dx - 1], xc_send, xc_recv, at((x + dx) % 4, zh, slot))

    def zc_copy(dx):
        return remote(zcs.at[dx], zcr.at[dx], zc_send, zc_recv, at((x + dx) % 4, 1 - zh, slot))

    def body(i, carry):
        @pl.when(i < CHUNKS)
        def _():
            n = chunk_of(i, x, zh)[2]

            @pl.when(i >= 2)
            def _():
                wait_recv(xall.at[n, 1 - c], f_recv.at[i])

            for b in range(4):
                rows = pl.ds(16 * b, 16)
                squares = 0.0
                for h in range(2):
                    feats = xall[n, h, rows, :].astype(F32)
                    xg[h, rows, :] = (feats * gain_ref[:, pl.ds(1024 * h, 1024)]).astype(BF16)
                    squares = squares + jnp.sum(feats * feats, axis=1, keepdims=True)
                col[rows, :] = jnp.broadcast_to(squares, (16, 128))
            ssr[4 * i + zl] = col[...].T[:8]

            @pl.when((middle == 0) & (i < AT_ENDS))
            def _():
                ss_copy(i, far_end).start()

            @pl.when((middle == 0) & (i >= AT_ENDS))
            def _():
                ss_copy(i, here).start()
                ss_copy(i, across).start()

            @pl.when((middle == 1) & (i < AT_ENDS))
            def _():
                ss_copy(i, near_end).start()
                ss_copy(i, far_end).start()

            @pl.when((middle == 1) & (i >= AT_ENDS))
            def _():
                ss_copy(i, across).start()

            for t in range(5):
                cols = pl.ds(t * 256, 256)
                tile = jnp.dot(xg[0], wgu[pl.ds(0, 1024), cols], preferred_element_type=F32) + jnp.dot(
                    xg[1], wgu[pl.ds(1024, 1024), cols], preferred_element_type=F32
                )
                for half in range(2):
                    part[i, half, :, cols] = tile[half * PART : (half + 1) * PART]

            @pl.when(middle == 0)
            def _():
                pout[2 * i + side] = part[i, side].astype(BF16)
                p_copy(i, side, here).start()

                @pl.when(i >= AT_ENDS)
                def _():
                    pout[2 * i + 1 - side] = part[i, 1 - side].astype(BF16)
                    p_copy(i, 1 - side, here).start()

        k = i - 6

        @pl.when((middle == 1) & (k >= 0) & (k < AT_ENDS))
        def _():
            wait_recv(hbuf.at[k, 1 - side], e_recv.at[k])
            h_copy(k, 1 - side, 0, across).start()

        k = i - 3

        @pl.when((middle == 1) & (k >= 0) & (k < AT_ENDS))
        def _():
            wait_recv(min_.at[k], m_recv.at[k])
            pout[2 * k + 1 - side] = (part[k, 1 - side] + min_[k].astype(F32)).astype(BF16)
            p_copy(k, 1 - side, near_end).start()

        @pl.when((middle == 1) & (k >= AT_ENDS) & (k < CHUNKS))
        def _():
            activate(k)
            h_copy(k, 1 - side, 0, across).start()
            h_copy(k, 1 - side, 2, far_end).start()
            h_copy(k, 1 - side, 1, near_end).start()

        u = i - 1

        @pl.when((middle == 1) & (u >= 0) & (u < CHUNKS))
        def _():
            wait_recv(pin.at[0], p_recv.at[u, side])
            mout[u] = (part[u, side] + pin[2 * u + side].astype(F32)).astype(BF16)
            m_copy(u).start()

        k = i - 4

        @pl.when((middle == 0) & (k >= 0) & (k < AT_ENDS))
        def _():
            activate(k)
            end_h_copy(k).start()

        def down(late, carry):
            j = i - 8 + middle + 2 * late

            @pl.when((j >= AT_ENDS * late) & (j < AT_ENDS + (CHUNKS - AT_ENDS) * late))
            def _():
                @pl.when((middle == 0) & (j >= AT_ENDS))
                def _():
                    wait_recv(hbuf.at[j], h_recv.at[j])

                @pl.when((middle == 1) | (j < AT_ENDS))
                def _():
                    wait_recv(hbuf.at[j, side], h_recv.at[j])

                @pl.when((middle == 1) & (j < AT_ENDS))
                def _():
                    h_copy(j, side, 1, near_end).start()

                hidden = jnp.concatenate([hbuf[j, 0], hbuf[j, 1]], axis=0)
                for t in range(4):
                    left = jnp.dot(hidden, wd[:, pl.ds(t * 256, 256)], preferred_element_type=F32)
                    right = jnp.dot(hidden, wd[:, pl.ds(1024 + t * 256, 256)], preferred_element_type=F32)
                    for b in range(8):
                        block = jnp.concatenate([left[b * 8 : b * 8 + 8], right[b * 8 : b * 8 + 8]], axis=0)
                        cs[j, b % 2, b // 2, :, pl.ds(t * 256, 256)] = block.astype(BF16)
                s_copy(j).start()

            return carry

        lax.fori_loop(0, 2, down, 0)

        def pair(late, carry):
            j = i - 9 + middle + 2 * late

            @pl.when((j >= AT_ENDS * late) & (j < AT_ENDS + (CHUNKS - AT_ENDS) * late))
            def _():
                wait_recv(sr.at[j], s_recv.at[j])
                for b in range(4):
                    cy[j, b] = (cs[j, c, b].astype(F32) + sr[j, b].astype(F32)).astype(BF16)
                for d in range(1, 4):
                    c_copy(j, d).start()
                cr[j, y] = cy[j, y]

            return carry

        lax.fori_loop(0, 2, pair, 0)

        m = i - 11 + middle

        @pl.when((m >= 0) & (m < CHUNKS))
        def _():
            wait_recv(cr.at[m, pl.ds(0, 3)], c_recv.at[m])
            total = cr[m, 0].astype(F32)
            for b in range(1, 4):
                total = total + cr[m, b].astype(F32)
            dx, flip, _ = chunk_of(m, x, zh)

            @pl.when(m == 0)
            def _():
                acc[...] = total

            @pl.when((m > 0) & (flip == 0))
            def _():
                xcs[dx - 1] = total.astype(BF16)
                xc_copy(dx).start()

            @pl.when(flip == 1)
            def _():
                zcs[dx] = total.astype(BF16)
                zc_copy(dx).start()

        @pl.when(i == 0)
        def _():
            assemble(1)

        for when, ready in ((1, (2, 3)), (2, (7,)), (3, (4, 5)), (4, (6,))):

            @pl.when(i == when)
            def _():
                for j in ready:
                    n = chunk_of(j, x, zh)[2]
                    wait_recv(xall.at[n, c], x_recv.at[n])
                    forward(j).start()

        return carry

    lax.fori_loop(0, CHUNKS + 11, body, 0)

    wait_recv(zcr, zc_recv)
    total = acc[...]
    for dx in range(4):
        total = total + zcr[dx].astype(F32)
    wait_recv(xcr, xc_recv)
    for dx in range(3):
        total = total + xcr[dx].astype(F32)
    out_ref[...] = jnp.concatenate([total[:8], total[8:]], axis=1).astype(BF16)

    z_copy.wait_send()
    wait_send(xblk.at[:, pl.ds(0, 7)], y_send)
    wait_send(xall.at[pl.ds(0, 6), 0], x_send)
    wait_send(xall.at[pl.ds(0, 6), 0], f_send)
    wait_send(cs.at[:, 0], s_send)
    wait_send(cy.at[:, pl.ds(0, 3)], c_send)
    wait_send(xcs, xc_send)
    wait_send(zcs, zc_send)

    @pl.when(middle == 0)
    def _():
        wait_send(pout.at[pl.ds(0, 2 * CHUNKS - AT_ENDS)], p_send)
        wait_send(ssr.at[pl.ds(0, 2 * CHUNKS - AT_ENDS)], ss_send)
        wait_send(hbuf.at[pl.ds(0, AT_ENDS), 0], h_send.at[0])

    @pl.when(middle == 1)
    def _():
        wait_send(pout.at[pl.ds(0, AT_ENDS)], p_send)
        wait_send(ssr.at[pl.ds(0, CHUNKS + AT_ENDS)], ss_send)
        wait_send(mout, m_send)
        wait_send(hbuf.at[:, 0], h_send.at[0])
        wait_send(hbuf.at[:, 0], h_send.at[1])
        wait_send(hbuf.at[pl.ds(0, CHUNKS - AT_ENDS), 0], h_send.at[2])


def local(queries, cache_keys, value_cache, new_keys, token_values, lengths, norm_gain, w_gate, w_up, w_down):
    vmem = pl.BlockSpec(memory_space=pltpu.VMEM)
    hbm = pl.BlockSpec(memory_space=pltpu.HBM)
    dma = pltpu.SemaphoreType.DMA
    return pl.pallas_call(
        kernel,
        out_shape=(jax.ShapeDtypeStruct((8, 2048), BF16), jax.ShapeDtypeStruct((8, 2048), BF16)),
        in_specs=[hbm] * 10,
        out_specs=(vmem, vmem),
        scratch_shapes=[
            pltpu.VMEM((8, 2048), BF16),
            pltpu.VMEM((8, 128), BF16),
            pltpu.VMEM((8, 128), BF16),
            pltpu.SMEM((8,), jnp.int32),
            pltpu.VMEM((1, 2048), F32),
            pltpu.VMEM((8, 512, 128), BF16),
            pltpu.VMEM((8, 512, 128), BF16),
            pltpu.VMEM((2048, 2 * UNITS), BF16),
            pltpu.VMEM((UNITS, 2048), BF16),
            pltpu.VMEM((128, 128), F32),
            pltpu.VMEM((128, 128), F32),
            pltpu.VMEM((128, 128), F32),
            pltpu.VMEM((128, 128), F32),
            pltpu.VMEM((PART, 2 * UNITS), F32),
            pltpu.VMEM((4 * CHUNKS, 8, 128), F32),
            pltpu.VMEM((2, 8, 16, 1024), BF16),
            pltpu.VMEM((CHUNKS, 2, ROWS, 1024), BF16),
            pltpu.VMEM((2, ROWS, 1024), BF16),
            pltpu.VMEM((CHUNKS, 2, PART, 2 * UNITS), F32),
            pltpu.VMEM((2 * CHUNKS, PART, 2 * UNITS), BF16),
            pltpu.VMEM((2 * CHUNKS, PART, 2 * UNITS), BF16),
            pltpu.VMEM((CHUNKS, PART, 2 * UNITS), BF16),
            pltpu.VMEM((CHUNKS, PART, 2 * UNITS), BF16),
            pltpu.VMEM((CHUNKS, 2, PART, UNITS), BF16),
            pltpu.VMEM((CHUNKS, 2, 4, 16, 1024), BF16),
            pltpu.VMEM((CHUNKS, 4, 16, 1024), BF16),
            pltpu.VMEM((CHUNKS, 4, 16, 1024), BF16),
            pltpu.VMEM((CHUNKS, 4, 16, 1024), BF16),
            pltpu.VMEM((16, 1024), F32),
            pltpu.VMEM((3, 16, 1024), BF16),
            pltpu.VMEM((3, 16, 1024), BF16),
            pltpu.VMEM((4, 16, 1024), BF16),
            pltpu.VMEM((4, 16, 1024), BF16),
            dma((10,)),
            dma, dma((CHUNKS,)),
            dma, dma,
            dma, dma((2,)),
            dma, dma((CHUNKS,)),
            dma, dma((CHUNKS,)),
            dma, dma((CHUNKS, 2)),
            dma, dma((CHUNKS,)),
            dma((CHUNKS,)),
            dma((3,)), dma((CHUNKS,)),
            dma, dma((CHUNKS,)),
            dma, dma((CHUNKS,)),
            dma, dma,
            dma, dma,
        ],
        compiler_params=pltpu.CompilerParams(
            collective_id=0, has_side_effects=True, vmem_limit_bytes=60 * 1024 * 1024
        ),
    )(queries, new_keys, token_values, lengths, norm_gain.reshape(1, 2048), cache_keys, value_cache, w_gate, w_up, w_down)


def solution(mesh):
    in_specs = (
        P("attn", "ffn"),
        P("attn", None, "ffn"),
        P("attn", None, "ffn"),
        P("attn", "ffn"),
        P("attn", "ffn"),
        P("attn"),
        P("ffn"),
        P("ffn", "attn"),
        P("ffn", "attn"),
        P("attn", "ffn"),
    )
    out_specs = (P("attn", "ffn"), P("attn", "ffn"))
    return jax.shard_map(local, mesh=mesh, in_specs=in_specs, out_specs=out_specs, check_vma=False)
```

```python
import functools

import jax
import jax.numpy as jnp
from jax import lax
from jax.experimental import pallas as pl
from jax.experimental.pallas import tpu as pltpu
from jax.sharding import PartitionSpec as P

MESH = pl.DeviceIdType.MESH
F32, BF16 = jnp.float32, jnp.bfloat16
D = 8192
CHUNKS = 8
ROWS = 64
PART = 32
UNITS = 640
FORWARDED = 6
END_LAG = 7


def from_on(j, k):
    return (j + 8 - k) // 8


def chunk_of(j, x, zh):
    dx = from_on(j, 2) + from_on(j, 3) - from_on(j, 4) + from_on(j, 5) + from_on(j, 6)
    flip = from_on(j, 1) - from_on(j, 2) + from_on(j, 4) - from_on(j, 7)
    return dx, flip, ((x + dx) % 4) * 2 + (zh + flip) % 2


def kernel(
    q_hbm, nk_hbm, tv_hbm, len_hbm, gain_hbm, k_hbm, v_hbm, wg_hbm, wu_hbm, wd_hbm,
    out_ref,
    q_ref, nk_ref, tv_ref, len_ref, gain_ref, kbuf, vbuf, wgu, wd,
    qs, os, col, scales, sums, ssr, xblk, xall, xg, part, pout, pin, mout, min_, hbuf, cs, sr, cy, cr, acc, xcs, xcr, zcs, zcr,
    load_sem, ss_send, ss_recv, z_send, z_recv, y_send, y_recv, x_send, x_recv, f_send, f_recv,
    p_send, p_recv, m_send, m_recv, h_send, h_recv, s_send, s_recv, c_send, c_recv, xc_send, xc_recv, zc_send, zc_recv,
):
    a = lax.axis_index("attn")
    zl = lax.axis_index("ffn")
    c = a % 2
    y = (a // 2) % 4
    zh = (a // 8) % 2
    x = a // 16
    slot = y * 2 + c

    def at(x_, zh_, slot_, zl_=None):
        return {"attn": (x_ * 2 + zh_) * 8 + slot_, "ffn": zl if zl_ is None else zl_}

    sibling = at(x, zh, y * 2 + (1 - c))
    partner = at(x, 1 - zh, slot)

    def remote(src, dst, send, recv, device):
        return pltpu.make_async_remote_copy(
            src_ref=src, dst_ref=dst, send_sem=send, recv_sem=recv, device_id=device, device_id_type=MESH
        )

    pairs = [
        (q_hbm, q_ref), (nk_hbm, nk_ref), (len_hbm, len_ref), (k_hbm, kbuf), (tv_hbm, tv_ref), (v_hbm, vbuf), (gain_hbm, gain_ref),
        (wg_hbm, wgu.at[:, pl.ds(0, UNITS)]), (wu_hbm, wgu.at[:, pl.ds(UNITS, UNITS)]), (wd_hbm, wd),
    ]
    loads = [pltpu.make_async_copy(src, dst, load_sem.at[n]) for n, (src, dst) in enumerate(pairs)]
    for load in loads[:7]:
        load.start()

    barrier = pltpu.get_barrier_semaphore()
    peers = [at(x, zh, (slot + d) % 8) for d in range(1, 8)]
    peers += [at((x + d) % 4, zh, slot) for d in range(1, 4)]
    peers += [at(x, zh, slot, (zl + d) % 4) for d in range(1, 4)]
    peers += [at((x + d) % 4, 1 - zh, slot) for d in range(4)]
    for peer in peers:
        pl.semaphore_signal(barrier, inc=1, device_id=peer, device_id_type=MESH)

    for load in loads[:7]:
        load.wait()
    for load in loads[7:]:
        load.start()
    qf = q_ref[...].astype(F32)
    for g in range(16):
        qs[pl.ds(g * 8, 8), :] = qf[:, g * 128 : (g + 1) * 128]
    nk = nk_ref[...].astype(F32)
    tv = tv_ref[...].astype(F32)
    scaling = 1.0 / 128**0.5
    position = lax.broadcasted_iota(jnp.int32, (16, 512), 1)
    for r in range(8):
        q = qs[pl.ds(r, 16, stride=8), :]
        scores = lax.dot_general(
            q.astype(BF16), kbuf[r], (((1,), (1,)), ((), ())), preferred_element_type=F32
        ) * scaling
        own = jnp.sum(q * nk[r : r + 1, :], axis=1, keepdims=True) * scaling
        live = position < len_ref[r]
        scores = jnp.where(live, scores, -1e30)
        largest = jnp.maximum(jnp.max(scores, axis=1, keepdims=True), own)
        weights = jnp.where(live, jnp.exp(scores - largest), 0.0)
        own_weight = jnp.exp(own - largest)
        total = jnp.sum(weights, axis=1, keepdims=True) + own_weight
        probs = (weights / total).astype(BF16)
        own_prob = (own_weight / total).astype(BF16).astype(F32)
        out = jnp.dot(probs, vbuf[r], preferred_element_type=F32)
        os[pl.ds(r, 16, stride=8), :] = out + own_prob * tv[r : r + 1, :]
    attn = jnp.concatenate([os[pl.ds(g * 8, 8), :] for g in range(16)], axis=1).astype(BF16)
    out_ref[pl.ds(0, 8), :] = attn.astype(F32)
    feats = attn.astype(F32)
    xblk[0, slot] = jnp.concatenate([feats[:, :1024], feats[:, 1024:]], axis=0).astype(BF16)
    col[...] = jnp.zeros_like(col)

    pl.semaphore_wait(barrier, len(peers))

    z_copy = remote(xblk.at[0, slot], xblk.at[1, slot], z_send, z_recv, partner)
    z_copy.start()

    def y_copy(w, d):
        return remote(
            xblk.at[w, slot], xblk.at[w, slot], y_send, y_recv.at[w], at(x, zh, (slot + d) % 8)
        )

    def wait_send(ref, sem):
        remote(ref, ref, sem, sem, sibling).wait_send()

    def wait_recv(ref, sem):
        remote(ref, ref, sem, sem, sibling).wait_recv()

    def own_chunk(w):
        return x * 2 + (zh + w) % 2

    def x_copy(w, d):
        n = own_chunk(w)
        return remote(
            xall.at[n, c], xall.at[n, c], x_send, x_recv.at[n], at((x + d) % 4, zh, slot)
        )

    def assemble(w):
        n = own_chunk(w)
        wait_recv(xblk.at[w, pl.ds(0, 7)], y_recv.at[w])
        for b in range(4):
            first = xblk[w, 2 * b].astype(F32)
            second = xblk[w, 2 * b + 1].astype(F32)
            for h in range(2):
                pair = [first[8 * h : 8 * h + 8], second[8 * h : 8 * h + 8]]
                xall[n, h, pl.ds(16 * b, 16), :] = jnp.concatenate(pair, axis=0).astype(BF16)
        for d in range(1, 4):
            x_copy(w, d).start()

    for d in range(1, 8):
        y_copy(0, d).start()
    assemble(0)
    z_copy.wait_recv()
    for d in range(1, 8):
        y_copy(1, d).start()
    for load in loads[7:]:
        load.wait()

    side = zl // 2
    middle = zl * (3 - zl) // 2
    here = at(x, zh, slot, 1 + side)
    across = at(x, zh, slot, 2 - side)
    near_end = at(x, zh, slot, 3 * side)
    far_end = at(x, zh, slot, 3 - 3 * side)

    def p_copy(j, half, to):
        return remote(pout.at[2 * j + half], pin.at[2 * j + half], p_send, p_recv.at[j, half], to)

    def m_copy(j):
        return remote(mout.at[j], min_.at[j], m_send, m_recv.at[j], across)

    def ss_copy(j, to):
        return remote(ssr.at[4 * j + zl], ssr.at[4 * j + zl], ss_send, ss_recv.at[j], to)

    def h_copy(j, half, n, to):
        piece = hbuf.at[j, half]
        return remote(piece, piece, h_send.at[n], h_recv.at[j], to)

    def activate(j):
        wait_recv(ssr.at[pl.ds(0, 3)], ss_recv.at[j])
        squares = ssr[4 * j] + ssr[4 * j + 1] + ssr[4 * j + 2] + ssr[4 * j + 3]
        scale = lax.rsqrt(squares / D + 1e-05)
        scales[...] = jnp.broadcast_to(scale, (128, 128)).T
        scale = scales[pl.ds(pl.multiple_of((1 - side) * PART, PART), PART), :][:, :1]
        wait_recv(pin.at[0], p_recv.at[j, 1 - side])
        wait_recv(min_.at[j], m_recv.at[j])
        sums[...] = part[j, 1 - side] + pin[2 * j + 1 - side].astype(F32) + min_[j].astype(F32)
        gate, up = sums[:, pl.ds(0, UNITS)] * scale, sums[:, pl.ds(UNITS, UNITS)] * scale
        hidden = gate / (1.0 + jnp.exp(-gate)) * up
        hbuf[j, 1 - side] = hidden.astype(BF16)

    def forward(j):
        n = chunk_of(j, x, zh)[2]
        return remote(xall.at[n, c], xall.at[n, c], f_send, f_recv.at[j], sibling)

    def s_copy(j):
        return remote(cs.at[j, 1 - c], sr.at[j], s_send, s_recv.at[j], sibling)

    def c_copy(j, d):
        to = (y + d) % 4
        return remote(cy.at[j, to], cr.at[j, y], c_send, c_recv.at[j], at(x, zh, to * 2 + c))

    def xc_copy(dx):
        return remote(xcs.at[dx - 1], xcr.at[dx - 1], xc_send, xc_recv, at((x + dx) % 4, zh, slot))

    def zc_copy(dx):
        return remote(zcs.at[dx], zcr.at[dx], zc_send, zc_recv, at((x + dx) % 4, 1 - zh, slot))

    def body(i, carry):
        lag = 4 + (END_LAG - 4) * (1 - middle)

        @pl.when(i < CHUNKS)
        def _():
            n = chunk_of(i, x, zh)[2]

            @pl.when(i >= 2)
            def _():
                wait_recv(xall.at[n, 1 - c], f_recv.at[i])

            for b in range(4):
                rows = pl.ds(16 * b, 16)
                squares = 0.0
                for h in range(2):
                    feats = xall[n, h, rows, :].astype(F32)
                    xg[h, rows, :] = (feats * gain_ref[:, pl.ds(1024 * h, 1024)]).astype(BF16)
                    squares = squares + jnp.sum(feats * feats, axis=1, keepdims=True)
                col[rows, :] = jnp.broadcast_to(squares, (16, 128))
            ssr[4 * i + zl] = col[...].T[:1]

            @pl.when(middle == 0)
            def _():
                ss_copy(i, here).start()
                ss_copy(i, across).start()

            @pl.when(middle == 1)
            def _():
                ss_copy(i, across).start()

            for t in range(5):
                cols = pl.ds(t * 256, 256)
                tile = jnp.dot(xg[0], wgu[pl.ds(0, 1024), cols], preferred_element_type=F32) + jnp.dot(
                    xg[1], wgu[pl.ds(1024, 1024), cols], preferred_element_type=F32
                )
                for half in range(2):
                    part[i, half, :, cols] = tile[half * PART : (half + 1) * PART]

            @pl.when(middle == 0)
            def _():
                for half in (side, 1 - side):
                    pout[2 * i + half] = part[i, half].astype(BF16)
                    p_copy(i, half, here).start()

        g = i - lag - 1

        @pl.when((g >= 0) & (g < CHUNKS))
        def _():
            wait_recv(sr.at[g], s_recv.at[g])
            for b in range(4):
                cy[g, b] = (cs[g, c, b].astype(F32) + sr[g, b].astype(F32)).astype(BF16)
            for d in range(1, 4):
                c_copy(g, d).start()
            cr[g, y] = cy[g, y]

        k = i - 3

        @pl.when((middle == 1) & (k >= 0) & (k < CHUNKS))
        def _():
            activate(k)
            h_copy(k, 1 - side, 0, across).start()
            h_copy(k, 1 - side, 1, near_end).start()

            @pl.when(k >= FORWARDED)
            def _():
                h_copy(k, 1 - side, 2, far_end).start()

        u = i - 1

        @pl.when((middle == 1) & (u >= 0) & (u < CHUNKS))
        def _():
            wait_recv(pin.at[0], p_recv.at[u, side])
            mout[u] = (part[u, side] + pin[2 * u + side].astype(F32)).astype(BF16)
            m_copy(u).start()

        j = i - lag

        @pl.when((j >= 0) & (j < CHUNKS))
        def _():
            @pl.when(middle == 0)
            def _():
                wait_recv(hbuf.at[j], h_recv.at[j])

            @pl.when(middle == 1)
            def _():
                wait_recv(hbuf.at[j, side], h_recv.at[j])

                @pl.when(j < FORWARDED)
                def _():
                    h_copy(j, side, 2, near_end).start()

            hidden = jnp.concatenate([hbuf[j, 0], hbuf[j, 1]], axis=0)
            for t in range(4):
                left = jnp.dot(hidden, wd[:, pl.ds(t * 256, 256)], preferred_element_type=F32)
                right = jnp.dot(hidden, wd[:, pl.ds(1024 + t * 256, 256)], preferred_element_type=F32)
                for b in range(8):
                    block = jnp.concatenate([left[b * 8 : b * 8 + 8], right[b * 8 : b * 8 + 8]], axis=0)
                    cs[j, b % 2, b // 2, :, pl.ds(t * 256, 256)] = block.astype(BF16)
            s_copy(j).start()

        m = i - lag - 2

        @pl.when((m >= 0) & (m < CHUNKS))
        def _():
            wait_recv(cr.at[m, pl.ds(0, 3)], c_recv.at[m])
            total = cr[m, 0].astype(F32)
            for b in range(1, 4):
                total = total + cr[m, b].astype(F32)
            dx, flip, _ = chunk_of(m, x, zh)

            @pl.when(m == 0)
            def _():
                acc[...] = total

            @pl.when((m > 0) & (flip == 0))
            def _():
                xcs[dx - 1] = total.astype(BF16)
                xc_copy(dx).start()

            @pl.when(flip == 1)
            def _():
                zcs[dx] = total.astype(BF16)
                zc_copy(dx).start()

        @pl.when(i == 0)
        def _():
            assemble(1)

        for when, ready in ((1, (2, 3)), (2, (7,)), (3, (4, 5)), (4, (6,))):

            @pl.when(i == when)
            def _():
                for j in ready:
                    n = chunk_of(j, x, zh)[2]
                    wait_recv(xall.at[n, c], x_recv.at[n])
                    forward(j).start()

        return carry

    lax.fori_loop(0, CHUNKS + END_LAG + 2, body, 0)

    wait_recv(zcr, zc_recv)
    total = acc[...]
    for dx in range(4):
        total = total + zcr[dx].astype(F32)
    wait_recv(xcr, xc_recv)
    for dx in range(3):
        total = total + xcr[dx].astype(F32)
    out_ref[pl.ds(8, 8), :] = jnp.concatenate([total[:8], total[8:]], axis=1)

    z_copy.wait_send()
    wait_send(xblk.at[:, pl.ds(0, 7)], y_send)
    wait_send(xall.at[pl.ds(0, 6), 0], x_send)
    wait_send(xall.at[pl.ds(0, 6), 0], f_send)
    wait_send(cs.at[:, 0], s_send)
    wait_send(cy.at[:, pl.ds(0, 3)], c_send)
    wait_send(xcs, xc_send)
    wait_send(zcs, zc_send)

    @pl.when(middle == 0)
    def _():
        wait_send(pout, p_send)
        wait_send(ssr.at[pl.ds(0, 2 * CHUNKS)], ss_send)

    @pl.when(middle == 1)
    def _():
        wait_send(ssr.at[pl.ds(0, CHUNKS)], ss_send)
        wait_send(mout, m_send)
        for n in range(3):
            wait_send(hbuf.at[:, 0], h_send.at[n])


def local(queries, cache_keys, value_cache, new_keys, token_values, lengths, norm_gain, w_gate, w_up, w_down):
    vmem = pl.BlockSpec(memory_space=pltpu.VMEM)
    hbm = pl.BlockSpec(memory_space=pltpu.HBM)
    dma = pltpu.SemaphoreType.DMA
    both = pl.pallas_call(
        kernel,
        out_shape=jax.ShapeDtypeStruct((16, 2048), F32),
        in_specs=[hbm] * 10,
        out_specs=vmem,
        scratch_shapes=[
            pltpu.VMEM((8, 2048), BF16),
            pltpu.VMEM((8, 128), BF16),
            pltpu.VMEM((8, 128), BF16),
            pltpu.SMEM((8,), jnp.int32),
            pltpu.VMEM((1, 2048), F32),
            pltpu.VMEM((8, 512, 128), BF16),
            pltpu.VMEM((8, 512, 128), BF16),
            pltpu.VMEM((2048, 2 * UNITS), BF16),
            pltpu.VMEM((UNITS, 2048), BF16),
            pltpu.VMEM((128, 128), F32),
            pltpu.VMEM((128, 128), F32),
            pltpu.VMEM((128, 128), F32),
            pltpu.VMEM((128, 128), F32),
            pltpu.VMEM((PART, 2 * UNITS), F32),
            pltpu.VMEM((4 * CHUNKS, 1, 128), F32),
            pltpu.VMEM((2, 8, 16, 1024), BF16),
            pltpu.VMEM((CHUNKS, 2, ROWS, 1024), BF16),
            pltpu.VMEM((2, ROWS, 1024), BF16),
            pltpu.VMEM((CHUNKS, 2, PART, 2 * UNITS), F32),
            pltpu.VMEM((2 * CHUNKS, PART, 2 * UNITS), BF16),
            pltpu.VMEM((2 * CHUNKS, PART, 2 * UNITS), BF16),
            pltpu.VMEM((CHUNKS, PART, 2 * UNITS), BF16),
            pltpu.VMEM((CHUNKS, PART, 2 * UNITS), BF16),
            pltpu.VMEM((CHUNKS, 2, PART, UNITS), BF16),
            pltpu.VMEM((CHUNKS, 2, 4, 16, 1024), BF16),
            pltpu.VMEM((CHUNKS, 4, 16, 1024), BF16),
            pltpu.VMEM((CHUNKS, 4, 16, 1024), BF16),
            pltpu.VMEM((CHUNKS, 4, 16, 1024), BF16),
            pltpu.VMEM((16, 1024), F32),
            pltpu.VMEM((3, 16, 1024), BF16),
            pltpu.VMEM((3, 16, 1024), BF16),
            pltpu.VMEM((4, 16, 1024), BF16),
            pltpu.VMEM((4, 16, 1024), BF16),
            dma((10,)),
            dma, dma((CHUNKS,)),
            dma, dma,
            dma, dma((2,)),
            dma, dma((CHUNKS,)),
            dma, dma((CHUNKS,)),
            dma, dma((CHUNKS, 2)),
            dma, dma((CHUNKS,)),
            dma((3,)), dma((CHUNKS,)),
            dma, dma((CHUNKS,)),
            dma, dma((CHUNKS,)),
            dma, dma,
            dma, dma,
        ],
        compiler_params=pltpu.CompilerParams(
            collective_id=0, has_side_effects=True, vmem_limit_bytes=60 * 1024 * 1024
        ),
    )(queries, new_keys, token_values, lengths, norm_gain.reshape(1, 2048), cache_keys, value_cache, w_gate, w_up, w_down)
    return both[:8].astype(BF16), both[8:].astype(BF16)


def solution(mesh):
    in_specs = (
        P("attn", "ffn"),
        P("attn", None, "ffn"),
        P("attn", None, "ffn"),
        P("attn", "ffn"),
        P("attn", "ffn"),
        P("attn"),
        P("ffn"),
        P("ffn", "attn"),
        P("ffn", "attn"),
        P("attn", "ffn"),
    )
    out_specs = (P("attn", "ffn"), P("attn", "ffn"))
    return jax.shard_map(local, mesh=mesh, in_specs=in_specs, out_specs=out_specs, check_vma=False)
```

```python
import functools

import jax
import jax.numpy as jnp
from jax import lax
from jax.experimental import pallas as pl
from jax.experimental.pallas import tpu as pltpu
from jax.sharding import PartitionSpec as P

MESH = pl.DeviceIdType.MESH
F32, BF16 = jnp.float32, jnp.bfloat16
D = 8192
CHUNKS = 8
ROWS = 64
PART = 32
UNITS = 640
FORWARDED = 6
END_LAG = 7


def from_on(j, k):
    return (j + 8 - k) // 8


def chunk_of(j, x, zh):
    dx = from_on(j, 2) + from_on(j, 3) - from_on(j, 4) + from_on(j, 5) + from_on(j, 6)
    flip = from_on(j, 1) - from_on(j, 2) + from_on(j, 4) - from_on(j, 7)
    return dx, flip, ((x + dx) % 4) * 2 + (zh + flip) % 2


def kernel(
    q_hbm, nk_hbm, tv_hbm, len_hbm, gain_hbm, k_hbm, v_hbm, wg_hbm, wu_hbm, wd_hbm,
    out_ref,
    q_ref, nk_ref, tv_ref, len_ref, gain_ref, kbuf, vbuf, wgu, wd,
    qs, os, col, scales, sums, ssr, xblk, xall, xg, part, pout, pin, mout, min_, hbuf, cs, sr, cy, cr, acc, xcs, xcr, zcs, zcr,
    load_sem, ss_send, ss_recv, z_send, z_recv, y_send, y_recv, x_send, x_recv, f_send, f_recv,
    p_send, p_recv, m_send, m_recv, h_send, h_recv, s_send, s_recv, c_send, c_recv, xc_send, xc_recv, zc_send, zc_recv,
):
    a = lax.axis_index("attn")
    zl = lax.axis_index("ffn")
    c = a % 2
    y = (a // 2) % 4
    zh = (a // 8) % 2
    x = a // 16
    slot = y * 2 + c

    def at(x_, zh_, slot_, zl_=None):
        return {"attn": (x_ * 2 + zh_) * 8 + slot_, "ffn": zl if zl_ is None else zl_}

    sibling = at(x, zh, y * 2 + (1 - c))
    partner = at(x, 1 - zh, slot)

    def remote(src, dst, send, recv, device):
        return pltpu.make_async_remote_copy(
            src_ref=src, dst_ref=dst, send_sem=send, recv_sem=recv, device_id=device, device_id_type=MESH
        )

    pairs = [
        (q_hbm, q_ref), (nk_hbm, nk_ref), (len_hbm, len_ref), (k_hbm, kbuf), (tv_hbm, tv_ref), (v_hbm, vbuf), (gain_hbm, gain_ref),
        (wg_hbm, wgu.at[:, pl.ds(0, UNITS)]), (wu_hbm, wgu.at[:, pl.ds(UNITS, UNITS)]), (wd_hbm, wd),
    ]
    loads = [pltpu.make_async_copy(src, dst, load_sem.at[n]) for n, (src, dst) in enumerate(pairs)]
    for load in loads[:7]:
        load.start()

    barrier = pltpu.get_barrier_semaphore()
    peers = [at(x, zh, (slot + d) % 8) for d in range(1, 8)]
    peers += [at((x + d) % 4, zh, slot) for d in range(1, 4)]
    peers += [at(x, zh, slot, (zl + d) % 4) for d in range(1, 4)]
    peers += [at((x + d) % 4, 1 - zh, slot) for d in range(4)]
    for peer in peers:
        pl.semaphore_signal(barrier, inc=1, device_id=peer, device_id_type=MESH)

    for load in loads[:7]:
        load.wait()
    for load in loads[7:]:
        load.start()
    qf = q_ref[...].astype(F32)
    for g in range(16):
        qs[pl.ds(g * 8, 8), :] = qf[:, g * 128 : (g + 1) * 128]
    nk = nk_ref[...].astype(F32)
    tv = tv_ref[...].astype(F32)
    scaling = 1.0 / 128**0.5
    position = lax.broadcasted_iota(jnp.int32, (16, 512), 1)
    for r in range(8):
        q = qs[pl.ds(r, 16, stride=8), :]
        scores = lax.dot_general(
            q.astype(BF16), kbuf[r], (((1,), (1,)), ((), ())), preferred_element_type=F32
        ) * scaling
        own = jnp.sum(q * nk[r : r + 1, :], axis=1, keepdims=True) * scaling
        live = position < len_ref[r]
        scores = jnp.where(live, scores, -1e30)
        largest = jnp.maximum(jnp.max(scores, axis=1, keepdims=True), own)
        weights = jnp.where(live, jnp.exp(scores - largest), 0.0)
        own_weight = jnp.exp(own - largest)
        total = jnp.sum(weights, axis=1, keepdims=True) + own_weight
        probs = (weights / total).astype(BF16)
        own_prob = (own_weight / total).astype(BF16).astype(F32)
        out = jnp.dot(probs, vbuf[r], preferred_element_type=F32)
        os[pl.ds(r, 16, stride=8), :] = out + own_prob * tv[r : r + 1, :]
    attn = jnp.concatenate([os[pl.ds(g * 8, 8), :] for g in range(16)], axis=1).astype(BF16)
    out_ref[pl.ds(0, 8), :] = attn.astype(F32)
    feats = attn.astype(F32)
    xblk[0, slot] = jnp.concatenate([feats[:, :1024], feats[:, 1024:]], axis=0).astype(BF16)
    col[...] = jnp.zeros_like(col)

    pl.semaphore_wait(barrier, len(peers))

    z_copy = remote(xblk.at[0, slot], xblk.at[1, slot], z_send, z_recv, partner)
    z_copy.start()

    def y_copy(w, d):
        return remote(
            xblk.at[w, slot], xblk.at[w, slot], y_send, y_recv.at[w], at(x, zh, (slot + d) % 8)
        )

    def wait_send(ref, sem):
        remote(ref, ref, sem, sem, sibling).wait_send()

    def wait_recv(ref, sem):
        remote(ref, ref, sem, sem, sibling).wait_recv()

    def own_chunk(w):
        return x * 2 + (zh + w) % 2

    def x_copy(w, d):
        n = own_chunk(w)
        return remote(
            xall.at[n, c], xall.at[n, c], x_send, x_recv.at[n], at((x + d) % 4, zh, slot)
        )

    def assemble(w):
        n = own_chunk(w)
        wait_recv(xblk.at[w, pl.ds(0, 7)], y_recv.at[w])
        for b in range(4):
            first = xblk[w, 2 * b].astype(F32)
            second = xblk[w, 2 * b + 1].astype(F32)
            for h in range(2):
                pair = [first[8 * h : 8 * h + 8], second[8 * h : 8 * h + 8]]
                xall[n, h, pl.ds(16 * b, 16), :] = jnp.concatenate(pair, axis=0).astype(BF16)
        for d in range(1, 4):
            x_copy(w, d).start()

    for d in range(1, 8):
        y_copy(0, d).start()
    assemble(0)
    z_copy.wait_recv()
    for d in range(1, 8):
        y_copy(1, d).start()
    for load in loads[7:]:
        load.wait()

    side = zl // 2
    middle = zl * (3 - zl) // 2
    here = at(x, zh, slot, 1 + side)
    across = at(x, zh, slot, 2 - side)
    near_end = at(x, zh, slot, 3 * side)
    far_end = at(x, zh, slot, 3 - 3 * side)

    def p_copy(j, half, to):
        return remote(pout.at[2 * j + half], pin.at[2 * j + half], p_send, p_recv.at[j, half], to)

    def m_copy(j):
        return remote(mout.at[j], min_.at[j], m_send, m_recv.at[j], across)

    def ss_copy(j, to):
        return remote(ssr.at[4 * j + zl], ssr.at[4 * j + zl], ss_send, ss_recv.at[j], to)

    def h_copy(j, half, n, to):
        piece = hbuf.at[j, half]
        return remote(piece, piece, h_send.at[n], h_recv.at[j], to)

    def activate(j):
        wait_recv(ssr.at[pl.ds(0, 3)], ss_recv.at[j])
        squares = ssr[4 * j] + ssr[4 * j + 1] + ssr[4 * j + 2] + ssr[4 * j + 3]
        scale = lax.rsqrt(squares / D + 1e-05)
        scales[...] = jnp.broadcast_to(scale, (128, 128)).T
        scale = scales[pl.ds(pl.multiple_of((1 - side) * PART, PART), PART), :][:, :1]
        wait_recv(pin.at[0], p_recv.at[j, 1 - side])
        wait_recv(min_.at[j], m_recv.at[j])
        sums[...] = part[j, 1 - side] + pin[2 * j + 1 - side].astype(F32) + min_[j].astype(F32)
        gate, up = sums[:, pl.ds(0, UNITS)] * scale, sums[:, pl.ds(UNITS, UNITS)] * scale
        hidden = gate / (1.0 + jnp.exp(-gate)) * up
        hbuf[j, 1 - side] = hidden.astype(BF16)

    def forward(j):
        n = chunk_of(j, x, zh)[2]
        return remote(xall.at[n, c], xall.at[n, c], f_send, f_recv.at[j], sibling)

    def s_copy(j):
        return remote(cs.at[j, 1 - c], sr.at[j], s_send, s_recv.at[j], sibling)

    def c_copy(j, d):
        to = (y + d) % 4
        return remote(cy.at[j, to], cr.at[j, y], c_send, c_recv.at[j], at(x, zh, to * 2 + c))

    def xc_copy(dx):
        return remote(xcs.at[dx - 1], xcr.at[dx - 1], xc_send, xc_recv, at((x + dx) % 4, zh, slot))

    def zc_copy(dx):
        return remote(zcs.at[dx], zcr.at[dx], zc_send, zc_recv, at((x + dx) % 4, 1 - zh, slot))

    def body(i, carry):
        lag = 4 + (END_LAG - 4) * (1 - middle)

        @pl.when(i < CHUNKS)
        def _():
            n = chunk_of(i, x, zh)[2]

            @pl.when(i >= 2)
            def _():
                wait_recv(xall.at[n, 1 - c], f_recv.at[i])

            for b in range(4):
                rows = pl.ds(16 * b, 16)
                squares = 0.0
                for h in range(2):
                    feats = xall[n, h, rows, :].astype(F32)
                    xg[h, rows, :] = (feats * gain_ref[:, pl.ds(1024 * h, 1024)]).astype(BF16)
                    squares = squares + jnp.sum(feats * feats, axis=1, keepdims=True)
                col[rows, :] = jnp.broadcast_to(squares, (16, 128))
            ssr[4 * i + zl] = col[...].T[:1]

            @pl.when(middle == 0)
            def _():
                ss_copy(i, here).start()
                ss_copy(i, across).start()

            @pl.when(middle == 1)
            def _():
                ss_copy(i, across).start()

            for t in range(5):
                cols = pl.ds(t * 256, 256)
                tile = jnp.dot(xg[0], wgu[pl.ds(0, 1024), cols], preferred_element_type=F32) + jnp.dot(
                    xg[1], wgu[pl.ds(1024, 1024), cols], preferred_element_type=F32
                )
                for half in range(2):
                    part[i, half, :, cols] = tile[half * PART : (half + 1) * PART]

            @pl.when(middle == 0)
            def _():
                for half in (side, 1 - side):
                    pout[2 * i + half] = part[i, half].astype(BF16)
                    p_copy(i, half, here).start()

        g = i - lag - 1

        @pl.when((g >= 0) & (g < CHUNKS))
        def _():
            wait_recv(sr.at[g], s_recv.at[g])
            for b in range(4):
                cy[g, b] = (cs[g, c, b].astype(F32) + sr[g, b].astype(F32)).astype(BF16)
            for d in range(1, 4):
                c_copy(g, d).start()
            cr[g, y] = cy[g, y]

        k = i - 3

        @pl.when((middle == 1) & (k >= 0) & (k < CHUNKS))
        def _():
            activate(k)
            h_copy(k, 1 - side, 0, across).start()
            h_copy(k, 1 - side, 1, near_end).start()

            @pl.when(k >= FORWARDED)
            def _():
                h_copy(k, 1 - side, 2, far_end).start()

        j = i - lag

        @pl.when((j >= 0) & (j < CHUNKS))
        def _():
            @pl.when(middle == 0)
            def _():
                wait_recv(hbuf.at[j], h_recv.at[j])

            @pl.when(middle == 1)
            def _():
                wait_recv(hbuf.at[j, side], h_recv.at[j])

                @pl.when(j < FORWARDED)
                def _():
                    h_copy(j, side, 2, near_end).start()

            hidden = jnp.concatenate([hbuf[j, 0], hbuf[j, 1]], axis=0)
            for t in range(4):
                left = jnp.dot(hidden, wd[:, pl.ds(t * 256, 256)], preferred_element_type=F32)
                right = jnp.dot(hidden, wd[:, pl.ds(1024 + t * 256, 256)], preferred_element_type=F32)
                for b in range(8):
                    block = jnp.concatenate([left[b * 8 : b * 8 + 8], right[b * 8 : b * 8 + 8]], axis=0)
                    cs[j, b % 2, b // 2, :, pl.ds(t * 256, 256)] = block.astype(BF16)
            s_copy(j).start()

        u = i - 1

        @pl.when((middle == 1) & (u >= 0) & (u < CHUNKS))
        def _():
            wait_recv(pin.at[0], p_recv.at[u, side])
            mout[u] = (part[u, side] + pin[2 * u + side].astype(F32)).astype(BF16)
            m_copy(u).start()

        m = i - lag - 2

        @pl.when((m >= 0) & (m < CHUNKS))
        def _():
            wait_recv(cr.at[m, pl.ds(0, 3)], c_recv.at[m])
            total = cr[m, 0].astype(F32)
            for b in range(1, 4):
                total = total + cr[m, b].astype(F32)
            dx, flip, _ = chunk_of(m, x, zh)

            @pl.when(m == 0)
            def _():
                acc[...] = total

            @pl.when((m > 0) & (flip == 0))
            def _():
                xcs[dx - 1] = total.astype(BF16)
                xc_copy(dx).start()

            @pl.when(flip == 1)
            def _():
                zcs[dx] = total.astype(BF16)
                zc_copy(dx).start()

        @pl.when(i == 0)
        def _():
            assemble(1)

        for when, ready in ((1, (2, 3)), (2, (7,)), (3, (4, 5)), (4, (6,))):

            @pl.when(i == when)
            def _():
                for j in ready:
                    n = chunk_of(j, x, zh)[2]
                    wait_recv(xall.at[n, c], x_recv.at[n])
                    forward(j).start()

        return carry

    lax.fori_loop(0, CHUNKS + END_LAG + 2, body, 0)

    wait_recv(zcr, zc_recv)
    total = acc[...]
    for dx in range(4):
        total = total + zcr[dx].astype(F32)
    wait_recv(xcr, xc_recv)
    for dx in range(3):
        total = total + xcr[dx].astype(F32)
    out_ref[pl.ds(8, 8), :] = jnp.concatenate([total[:8], total[8:]], axis=1)

    z_copy.wait_send()
    wait_send(xblk.at[:, pl.ds(0, 7)], y_send)
    wait_send(xall.at[pl.ds(0, 6), 0], x_send)
    wait_send(xall.at[pl.ds(0, 6), 0], f_send)
    wait_send(cs.at[:, 0], s_send)
    wait_send(cy.at[:, pl.ds(0, 3)], c_send)
    wait_send(xcs, xc_send)
    wait_send(zcs, zc_send)

    @pl.when(middle == 0)
    def _():
        wait_send(pout, p_send)
        wait_send(ssr.at[pl.ds(0, 2 * CHUNKS)], ss_send)

    @pl.when(middle == 1)
    def _():
        wait_send(ssr.at[pl.ds(0, CHUNKS)], ss_send)
        wait_send(mout, m_send)
        for n in range(3):
            wait_send(hbuf.at[:, 0], h_send.at[n])


def local(queries, cache_keys, value_cache, new_keys, token_values, lengths, norm_gain, w_gate, w_up, w_down):
    vmem = pl.BlockSpec(memory_space=pltpu.VMEM)
    hbm = pl.BlockSpec(memory_space=pltpu.HBM)
    dma = pltpu.SemaphoreType.DMA
    both = pl.pallas_call(
        kernel,
        out_shape=jax.ShapeDtypeStruct((16, 2048), F32),
        in_specs=[hbm] * 10,
        out_specs=vmem,
        scratch_shapes=[
            pltpu.VMEM((8, 2048), BF16),
            pltpu.VMEM((8, 128), BF16),
            pltpu.VMEM((8, 128), BF16),
            pltpu.SMEM((8,), jnp.int32),
            pltpu.VMEM((1, 2048), F32),
            pltpu.VMEM((8, 512, 128), BF16),
            pltpu.VMEM((8, 512, 128), BF16),
            pltpu.VMEM((2048, 2 * UNITS), BF16),
            pltpu.VMEM((UNITS, 2048), BF16),
            pltpu.VMEM((128, 128), F32),
            pltpu.VMEM((128, 128), F32),
            pltpu.VMEM((128, 128), F32),
            pltpu.VMEM((128, 128), F32),
            pltpu.VMEM((PART, 2 * UNITS), F32),
            pltpu.VMEM((4 * CHUNKS, 1, 128), F32),
            pltpu.VMEM((2, 8, 16, 1024), BF16),
            pltpu.VMEM((CHUNKS, 2, ROWS, 1024), BF16),
            pltpu.VMEM((2, ROWS, 1024), BF16),
            pltpu.VMEM((CHUNKS, 2, PART, 2 * UNITS), F32),
            pltpu.VMEM((2 * CHUNKS, PART, 2 * UNITS), BF16),
            pltpu.VMEM((2 * CHUNKS, PART, 2 * UNITS), BF16),
            pltpu.VMEM((CHUNKS, PART, 2 * UNITS), BF16),
            pltpu.VMEM((CHUNKS, PART, 2 * UNITS), BF16),
            pltpu.VMEM((CHUNKS, 2, PART, UNITS), BF16),
            pltpu.VMEM((CHUNKS, 2, 4, 16, 1024), BF16),
            pltpu.VMEM((CHUNKS, 4, 16, 1024), BF16),
            pltpu.VMEM((CHUNKS, 4, 16, 1024), BF16),
            pltpu.VMEM((CHUNKS, 4, 16, 1024), BF16),
            pltpu.VMEM((16, 1024), F32),
            pltpu.VMEM((3, 16, 1024), BF16),
            pltpu.VMEM((3, 16, 1024), BF16),
            pltpu.VMEM((4, 16, 1024), BF16),
            pltpu.VMEM((4, 16, 1024), BF16),
            dma((10,)),
            dma, dma((CHUNKS,)),
            dma, dma,
            dma, dma((2,)),
            dma, dma((CHUNKS,)),
            dma, dma((CHUNKS,)),
            dma, dma((CHUNKS, 2)),
            dma, dma((CHUNKS,)),
            dma((3,)), dma((CHUNKS,)),
            dma, dma((CHUNKS,)),
            dma, dma((CHUNKS,)),
            dma, dma,
            dma, dma,
        ],
        compiler_params=pltpu.CompilerParams(
            collective_id=0, has_side_effects=True, vmem_limit_bytes=60 * 1024 * 1024
        ),
    )(queries, new_keys, token_values, lengths, norm_gain.reshape(1, 2048), cache_keys, value_cache, w_gate, w_up, w_down)
    return both[:8].astype(BF16), both[8:].astype(BF16)


def solution(mesh):
    in_specs = (
        P("attn", "ffn"),
        P("attn", None, "ffn"),
        P("attn", None, "ffn"),
        P("attn", "ffn"),
        P("attn", "ffn"),
        P("attn"),
        P("ffn"),
        P("ffn", "attn"),
        P("ffn", "attn"),
        P("attn", "ffn"),
    )
    out_specs = (P("attn", "ffn"), P("attn", "ffn"))
    return jax.shard_map(local, mesh=mesh, in_specs=in_specs, out_specs=out_specs, check_vma=False)
```
